32 devices in a mesh: groups: 2 (over x), seq: 16 (over z, y, core).
Axes of the slice: x: 2, y: 2, z: 4, core: 2. Of those that a mesh axis runs over, the one named last changes fastest.
Arguments:
- queries: bfloat16 [128, 8192], P(('groups', 'seq')), parts along dimension 0, may hold values from -15 to 15
- draft_keys: bfloat16 [128, 1024], P(('groups', 'seq')), parts along dimension 0, may hold values from -16 to 16
- draft_values: bfloat16 [128, 1024], P(('groups', 'seq')), parts along dimension 0, may hold values from -6 to 6
- parents: int32 [128], P(('groups', 'seq')), parts along dimension 0, may hold values from -1 to 2, as said below
- private_keys: bfloat16 [32, 1024, 1024], P(('groups', 'seq')), parts along dimension 0, may hold values from -8 to 8
- private_values: bfloat16 [32, 1024, 1024], P(('groups', 'seq')), parts along dimension 0, may hold values from -6 to 6
- priv_lengths: int32 [32], P(('groups', 'seq')), parts along dimension 0, may hold values from 1 to 1024, as said below
- prefix_keys: bfloat16 [32, 16384, 128], P(('groups', 'seq')), parts along dimension 0, may hold values from -8 to 8
- prefix_values: bfloat16 [32, 16384, 128], P(('groups', 'seq')), parts along dimension 0, may hold values from -6 to 6
- out_weight: bfloat16 [8192, 8192], P(None, 'seq'), may hold values from -0.0625 to 0.0625
Outputs:
- output: float32 [128, 8192], P(('groups', 'seq')), parts along dimension 0
The draws below stay inside these ranges and needn't reach their ends.
There are 2 independent parts, one for each index of `groups`. The reference program is written for one: setup_inputs(seed, part) draws one part's arguments, and reference() takes and returns one part's arrays. A program takes and returns all parts, laid end to end along the dimension named above; an argument that names none is the same for every part. Nothing has to cross between parts.
Inputs may be any that keep to these rules, and one draw needn't show every extreme that they name: parents[r * 4 + i] is the draft of request r that draft i extends, always smaller than i; -1 means draft i extends the cached context directly. Request r's live private slots are its first priv_lengths[r] slots; some request has all 1024.
All inputs are finite; a program needn't handle non-finite values.
Results may differ from the reference program's by a relative error of at most 0.0034.
Values may be sent and summed in bfloat16 or wider, within the bound.
A program may use at most 192 MiB of HBM per device.

```python
import jax
import jax.numpy as jnp
from jax import lax

D = 8192
HEADS = 64
KVH = 8
HD = 128
DRAFT = 4
PRIV = 1024
NBLK = 2
BLOCK = 16384
PREFIX = 32768
REQ = 16
ROWS = 64


def draw_queries(key, part):
    base_draw = jnp.clip(2.5 * jax.random.normal(jax.random.fold_in(key, 1), (ROWS, HEADS * HD), jnp.float32), -15.0, 15.0)
    return base_draw.astype(jnp.bfloat16)


def draw_prefix_keys(key, part):
    base_draw = jnp.clip(jax.random.normal(jax.random.fold_in(key, 2), (KVH * NBLK, BLOCK, HD), jnp.float32), -8.0, 8.0)
    return base_draw.astype(jnp.bfloat16)


def draw_parents(key, part):
    within = jnp.arange(ROWS, dtype=jnp.int32) % DRAFT
    picked = jax.random.randint(jax.random.fold_in(key, 3), (ROWS,), 0, DRAFT * 12)
    chosen = (picked % (within + 1) - 1).astype(jnp.int32)
    chain = (within - 1).astype(jnp.int32)
    return jnp.where(jnp.arange(ROWS, dtype=jnp.int32) < DRAFT, chain, chosen).astype(jnp.int32)


def draw_priv_lengths(key, part):
    lengths = jax.random.randint(jax.random.fold_in(key, 4), (REQ,), 1, PRIV + 1)
    longest = jax.random.randint(jax.random.fold_in(key, 5), (), 0, REQ)
    return lengths.at[longest].set(PRIV).astype(jnp.int32)


def block_levels(key, dims, cuts, smallest, largest):
    def one(axis_at, parts):
        heights = jax.random.uniform(jax.random.fold_in(jax.random.fold_in(key, 6), axis_at), (parts,), jnp.float32, smallest / len(cuts), largest / len(cuts))
        return jnp.repeat(jnp.exp(heights), dims[axis_at] // parts).reshape((-1,) + (1,) * (len(dims) - axis_at - 1))

    level = one(*cuts[0])
    for cut in cuts[1:]:
        level = level * one(*cut)
    return level


def normal_values(own_key, shape, spread, bound, shards=(), kind=jnp.bfloat16):
    entries = jax.random.normal(own_key, shape, jnp.float32) * spread
    if len(shards) > 0:
        entries = block_levels(own_key, shape, shards, -0.22, 0.18) * entries
    return jnp.clip(entries, min=-bound, max=bound).astype(kind)


def setup_inputs(seed: int = 0, part: int = 0) -> dict:
    streams_of = jax.random.split(jax.random.key(seed), 11)
    part_keys = jax.random.split(jax.random.fold_in(streams_of[10], part), 11)
    queries = draw_queries(jax.random.fold_in(jax.random.fold_in(streams_of[10], part), 71), part)
    draft_keys = normal_values(part_keys[1], (ROWS, KVH * HD), 3.0, 16.0, ((0, 16),))
    draft_values = normal_values(part_keys[2], (ROWS, KVH * HD), 1.0, 6.0, ((0, 16),))
    parents = draw_parents(jax.random.fold_in(jax.random.fold_in(streams_of[10], part), 71), part)
    private_keys = normal_values(part_keys[4], (REQ, PRIV, KVH * HD), 1.3, 8.0, ((0, 16),))
    private_values = normal_values(part_keys[5], (REQ, PRIV, KVH * HD), 1.0, 6.0, ((0, 16),))
    priv_lengths = draw_priv_lengths(jax.random.fold_in(jax.random.fold_in(streams_of[10], part), 71), part)
    prefix_keys = draw_prefix_keys(jax.random.fold_in(jax.random.fold_in(streams_of[10], part), 71), part)
    prefix_values = normal_values(part_keys[8], (KVH * NBLK, BLOCK, HD), 1.0, 6.0, ((0, 16),))
    out_weight = normal_values(streams_of[9], (HEADS * HD, D), (HEADS * HD) ** -0.5, 0.0625, ((1, 16),))
    return {"queries": queries, "draft_keys": draft_keys, "draft_values": draft_values, "parents": parents, "private_keys": private_keys, "private_values": private_values, "priv_lengths": priv_lengths, "prefix_keys": prefix_keys, "prefix_values": prefix_values, "out_weight": out_weight}


def tree_visible(parents):
    parent_rows = parents.reshape(-1, DRAFT).astype(jnp.int32)
    positions = jnp.arange(DRAFT, dtype=jnp.int32)
    visible = jnp.broadcast_to(positions[:, None] == positions[None, :], (parent_rows.shape[0], DRAFT, DRAFT))
    ancestor = parent_rows
    for repeat_step in range(DRAFT - 1):
        matched = ancestor[:, :, None] == positions[None, None, :]
        visible = visible | matched
        lifted = jnp.sum(jnp.where(matched, parent_rows[:, None, :], 0), axis=2).astype(jnp.int32)
        ancestor = jnp.where(ancestor >= 0, lifted, -1).astype(jnp.int32)
    return visible


def rounded(weights):
    return lax.optimization_barrier(weights.astype(jnp.bfloat16)).astype(jnp.float32)


def reference(queries, draft_keys, draft_values, parents, private_keys, private_values, priv_lengths, prefix_keys, prefix_values, out_weight):
    group_heads = HEADS // KVH
    score_scale = HD ** -0.5
    visible = tree_visible(parents)
    live_slots = jnp.arange(PRIV, dtype=jnp.int32)[None, :] < priv_lengths[:, None]
    key_heads = prefix_keys.reshape(KVH, PREFIX, HD)
    value_heads = prefix_values.reshape(KVH, PREFIX, HD)

    def one_group(group):
        query_cols = lax.dynamic_slice_in_dim(queries, group * (group_heads * HD), group_heads * HD, 1)
        flat_query = query_cols.reshape(ROWS * group_heads, HD)
        pre_keys = lax.dynamic_index_in_dim(key_heads, group, 0, keepdims=False)
        pre_vals = lax.dynamic_index_in_dim(value_heads, group, 0, keepdims=False)
        pre_scores = jnp.dot(flat_query, pre_keys.T, preferred_element_type=jnp.float32) * score_scale
        pre_scores = pre_scores.reshape(REQ, DRAFT, group_heads, PREFIX)
        query_four = query_cols.reshape(REQ, DRAFT, group_heads, HD).astype(jnp.float32)
        priv_keys = lax.dynamic_slice_in_dim(private_keys, group * HD, HD, 2).astype(jnp.float32)
        priv_vals = lax.dynamic_slice_in_dim(private_values, group * HD, HD, 2).astype(jnp.float32)
        draft_key = lax.dynamic_slice_in_dim(draft_keys, group * HD, HD, 1).reshape(REQ, DRAFT, HD).astype(jnp.float32)
        draft_val = lax.dynamic_slice_in_dim(draft_values, group * HD, HD, 1).reshape(REQ, DRAFT, HD).astype(jnp.float32)
        priv_scores = jnp.einsum('rihd,rkd->rihk', query_four, priv_keys) * score_scale
        priv_scores = jnp.where(live_slots[:, None, None, :], priv_scores, -1e30)
        tree_scores = jnp.einsum('rihd,rjd->rihj', query_four, draft_key) * score_scale
        tree_scores = jnp.where(visible[:, :, None, :], tree_scores, -1e30)
        row_max = jnp.maximum(jnp.max(pre_scores, axis=-1), jnp.maximum(jnp.max(priv_scores, axis=-1), jnp.max(tree_scores, axis=-1)))
        pre_w = jnp.exp(pre_scores - row_max[..., None])
        priv_w = jnp.exp(priv_scores - row_max[..., None])
        tree_w = jnp.exp(tree_scores - row_max[..., None])
        weight_sum = jnp.sum(pre_w, axis=-1) + jnp.sum(priv_w, axis=-1) + jnp.sum(tree_w, axis=-1)
        pre_mix = jnp.dot(pre_w.astype(jnp.bfloat16).reshape(ROWS * group_heads, PREFIX), pre_vals, preferred_element_type=jnp.float32)
        mixture = pre_mix.reshape(REQ, DRAFT, group_heads, HD)
        mixture = mixture + jnp.einsum('rihk,rkd->rihd', rounded(priv_w), priv_vals)
        mixture = mixture + jnp.einsum('rihj,rjd->rihd', rounded(tree_w), draft_val)
        return mixture / weight_sum[..., None]

    per_group = lax.map(one_group, jnp.arange(KVH, dtype=jnp.int32))
    attention = jnp.transpose(per_group, (1, 2, 0, 3, 4)).reshape(ROWS, HEADS * HD).astype(jnp.bfloat16)
    return jnp.dot(attention, out_weight, preferred_element_type=jnp.float32)
```

```python
import functools
import math

import jax
import jax.numpy as jnp
from jax import lax
from jax.experimental import pallas as pl
from jax.experimental.pallas import tpu as pltpu
from jax.sharding import PartitionSpec as P

HEADS = 64
KVH = 8
HD = 128
GH = HEADS // KVH
MESH = pl.DeviceIdType.MESH
F32 = jnp.float32
BF16 = jnp.bfloat16


def kernel(
    n,
    q_ref,
    dk_ref,
    dv_ref,
    par_ref,
    len_ref,
    pk_hbm,
    pv_hbm,
    k_hbm,
    v_hbm,
    w_hbm,
    o_ref,
    pk,
    pv,
    k,
    v,
    w,
    qf,
    qs,
    qbuf,
    dk_pad,
    dv_pad,
    priv_send,
    priv_buf,
    m_scr,
    part,
    merge_buf,
    fin,
    att,
    gat,
    acc,
    col,
    load_sem,
    q_ssem,
    q_rsem,
    p_ssem,
    p_rsem,
    m_ssem,
    m_rsem,
    g_ssem,
    g_rsem,
    o_ssem,
    o_rsem,
):
    me = lax.axis_index("seq")
    blocks = n // KVH
    lh = HEADS // n
    draft = q_ref.shape[0]
    gr = GH * draft
    lr = lh * draft
    lc = lh * HD
    cols = w.shape[1]
    g_me = me // blocks
    b_me = me % blocks
    c2 = HD**-0.5 * math.log2(math.e)

    loads = [
        pltpu.make_async_copy(pk_hbm.at[0], pk, load_sem.at[0]),
        pltpu.make_async_copy(pv_hbm.at[0], pv, load_sem.at[1]),
        pltpu.make_async_copy(k_hbm.at[0], k, load_sem.at[2]),
        pltpu.make_async_copy(v_hbm.at[0], v.at[:, pl.ds(0, HD)], load_sem.at[3]),
        pltpu.make_async_copy(w_hbm, w, load_sem.at[4]),
    ]
    for load in loads:
        load.start()

    def remote(src, dst, ssem, rsem, to):
        return pltpu.make_async_remote_copy(
            src_ref=src, dst_ref=dst, send_sem=ssem, recv_sem=rsem,
            device_id={"seq": to}, device_id_type=MESH,
        )

    barrier = pltpu.get_barrier_semaphore()
    for off in range(1, n):
        pl.semaphore_signal(
            barrier, inc=1, device_id={"seq": lax.rem(me + off, n)}, device_id_type=MESH
        )
    for g in range(KVH):
        for h in range(GH):
            at = (g * GH + h) * HD
            qf[g, h * draft : (h + 1) * draft, :] = q_ref[:, at : at + HD].astype(F32)
        qs[g] = qf[g].astype(BF16)
    dk_pad[...] = jnp.zeros_like(dk_pad)
    dv_pad[...] = jnp.zeros_like(dv_pad)
    dk_pad[0:draft, :] = dk_ref[...].astype(F32)
    dv_pad[0:draft, :] = dv_ref[...].astype(F32)
    qbuf[me] = qs[g_me]
    pl.semaphore_wait(barrier, n - 1)

    q_sends = []
    for off in range(1, n):
        to = lax.rem(me + off, n)
        q_sends.append(
            remote(qs.at[to // blocks], qbuf.at[me], q_ssem.at[off], q_rsem.at[me], to)
        )
        q_sends[-1].start()

    v[:, HD:] = jnp.ones((v.shape[0], HD), BF16)

    pad = dk_pad.shape[0]
    row_i = lax.broadcasted_iota(jnp.int32, (gr, pad), 0) % draft
    col_j = lax.broadcasted_iota(jnp.int32, (gr, pad), 1)
    seen = [[None] * draft for _ in range(draft)]
    visible = (row_i == col_j).astype(jnp.int32)
    for i in range(draft):
        for j in range(i):
            hit = (par_ref[i] == j).astype(jnp.int32)
            for mid in range(j + 1, i):
                hit = hit + (par_ref[i] == mid).astype(jnp.int32) * seen[mid][j]
            seen[i][j] = hit
            visible = jnp.where((row_i == i) & (col_j == j), hit, visible)
    slots = pk.shape[0]
    live = lax.broadcasted_iota(jnp.int32, (gr, slots), 1) < len_ref[0]
    lane = lax.broadcasted_iota(jnp.int32, (gr, HD), 1)
    loads[0].wait()
    loads[1].wait()
    nt = (((1,), (1,)), ((), ()))
    for g in range(KVH):
        cs = slice(g * HD, (g + 1) * HD)
        qg = qs[g]
        s = lax.dot_general(qg, pk[:, cs], nt, preferred_element_type=F32)
        t = lax.dot_general(qg, dk_pad[:, cs].astype(BF16), nt, preferred_element_type=F32)
        s = jnp.where(live, s, -1e30)
        t = jnp.where(visible > 0, t, -1e30)
        mx = jnp.maximum(
            jnp.max(s, axis=1, keepdims=True), jnp.max(t, axis=1, keepdims=True)
        )
        ps = jnp.exp2((s - mx) * c2)
        pt = jnp.exp2((t - mx) * c2)
        sm = jnp.sum(ps, axis=1, keepdims=True) + jnp.sum(pt, axis=1, keepdims=True)
        mix = jnp.dot(ps.astype(BF16), pv[:, cs], preferred_element_type=F32)
        mix = mix + jnp.dot(
            pt.astype(BF16), dv_pad[:, cs].astype(BF16), preferred_element_type=F32
        )
        priv_send[g, :, 0:HD] = mix
        priv_send[g, :, HD:] = jnp.where(lane == 0, mx, sm)

    def own_rows(b):
        return pl.ds(pl.multiple_of(b * lr, lr), lr)

    p_sends = []
    for off in range(1, n):
        to = lax.rem(me + off, n)
        p_sends.append(
            remote(
                priv_send.at[to // blocks, own_rows(to % blocks)], priv_buf.at[me],
                p_ssem.at[off], p_rsem.at[me], to,
            )
        )
        p_sends[-1].start()
    priv_buf[me] = priv_send[g_me, own_rows(b_me), :]

    for off in range(1, n):
        src = lax.rem(me + off, n)
        remote(qs.at[0], qbuf.at[src], q_ssem.at[off], q_rsem.at[src], src).wait_recv()
    loads[2].wait()
    loads[3].wait()
    rows = n * gr
    rb = 256
    ch = 2048
    reqs = rb // gr
    m_scr[...] = jnp.full_like(m_scr, -1e30)
    part[...] = jnp.zeros_like(part)

    def chunk(j, _):
        ks = pl.ds(pl.multiple_of(j * ch, ch), ch)
        kb = k[ks, :]
        vb = v[ks, :]
        for r in range(rows // rb):
            rs = slice(r * rb, (r + 1) * rb)
            qr = qbuf[r * reqs : (r + 1) * reqs].reshape(rb, HD)
            s = lax.dot_general(qr, kb, nt, preferred_element_type=F32)
            old = m_scr[rs, :]
            new = jnp.maximum(old, jnp.max(s, axis=1, keepdims=True))
            m_scr[rs, :] = new
            p = jnp.exp2((s - new[:, 0:1]) * c2).astype(BF16)
            fac = jnp.exp2((old - new) * c2)[:, 0:1]
            mix = jnp.dot(p, vb, preferred_element_type=F32)
            was = part[r * reqs : (r + 1) * reqs].reshape(rb, 2 * HD)
            part[r * reqs : (r + 1) * reqs] = (was * fac + mix).reshape(reqs, gr, 2 * HD)
        return 0

    lax.fori_loop(0, k.shape[0] // ch, chunk, 0)
    lane_m = lax.broadcasted_iota(jnp.int32, (n, gr, HD), 2)
    part[:, :, HD:] = jnp.where(lane_m == 0, m_scr[...].reshape(n, gr, HD), part[:, :, HD:])

    m_sends = []
    for off in range(1, blocks):
        b_to = lax.rem(b_me + off, blocks)
        m_sends.append(
            remote(
                part.at[:, own_rows(b_to)], merge_buf.at[b_me],
                m_ssem.at[off], m_rsem.at[b_me], g_me * blocks + b_to,
            )
        )
        m_sends[-1].start()
    for off in range(1, n):
        src = lax.rem(me + off, n)
        remote(
            priv_send.at[0, own_rows(0)], priv_buf.at[src], p_ssem.at[off], p_rsem.at[src], src
        ).wait_recv()
    pieces = [priv_buf[...], part[:, own_rows(b_me), :]]
    for off in range(1, blocks):
        b_src = lax.rem(b_me + off, blocks)
        remote(
            part.at[:, own_rows(0)], merge_buf.at[b_src],
            m_ssem.at[off], m_rsem.at[b_src], g_me * blocks + b_src,
        ).wait_recv()
        pieces.append(merge_buf[b_src])
    pieces = [x.reshape(n * lr, 2 * HD) for x in pieces]
    peak = functools.reduce(jnp.maximum, [x[:, HD : HD + 1] for x in pieces])
    facs = [jnp.exp2((x[:, HD : HD + 1] - peak) * c2) for x in pieces]
    den = sum(f * x[:, HD + 1 : HD + 2] for f, x in zip(facs, pieces))
    num = sum(f * x[:, 0:HD] for f, x in zip(facs, pieces))
    fin[...] = (num / den).reshape(n, lr, HD)
    for r in range(n):
        for h in range(lh):
            att[r * draft : (r + 1) * draft, h * HD : (h + 1) * HD] = fin[
                r, h * draft : (h + 1) * draft, :
            ]
    gat[me] = att[...].astype(BF16)

    core = me % 2
    chip = me // 2
    line = chip // 2
    side = chip % 2
    lines = n // 4

    def dev(line_at, side_at, core_at):
        return (line_at * 2 + side_at) * 2 + core_at

    g_sends = []

    def forward(src, to):
        g_sends.append(
            remote(gat.at[src], gat.at[src], g_ssem.at[len(g_sends)], g_rsem.at[src], to)
        )
        g_sends[-1].start()

    def arrived(src):
        remote(gat.at[src], gat.at[src], g_ssem.at[0], g_rsem.at[src], me ^ 1).wait_recv()

    def project(src):
        ws = pl.ds(pl.multiple_of(src * lc, lc), lc)
        return jnp.dot(gat[src], w[ws, :], preferred_element_type=F32)

    across = dev(line, 1 - side, core)
    partner = dev(line, side, 1 - core)
    forward(me, across)
    for off in range(1, lines):
        forward(me, dev(lax.rem(line + off, lines), side, core))
    forward(me, partner)
    loads[4].wait()
    acc[...] = project(me)
    for off in range(1, lines):
        src = dev(lax.rem(line + off, lines), side, core)
        arrived(src)
        forward(src, across)
        forward(src, partner)
        acc[...] += project(src)
    for off in range(lines):
        src = dev(lax.rem(line + off, lines), 1 - side, core)
        arrived(src)
        forward(src, partner)
        acc[...] += project(src)
    for side_at in (side, 1 - side):
        for off in range(lines):
            src = dev(lax.rem(line + off, lines), side_at, 1 - core)
            arrived(src)
            acc[...] += project(src)
    for r in range(n):
        col[r] = acc[r * draft : (r + 1) * draft, :]

    def out_cols(src):
        return o_ref.at[:, pl.ds(pl.multiple_of(src * cols, cols), cols)]

    o_sends = []
    for off in range(1, n):
        to = lax.rem(me + off, n)
        o_sends.append(
            remote(col.at[to], out_cols(me), o_ssem.at[off], o_rsem.at[me], to)
        )
        o_sends[-1].start()
    o_ref[:, pl.ds(pl.multiple_of(me * cols, cols), cols)] = col[me]
    for off in range(1, n):
        src = lax.rem(me + off, n)
        remote(col.at[0], out_cols(src), o_ssem.at[off], o_rsem.at[src], src).wait_recv()
    for sends in (q_sends, p_sends, m_sends, g_sends, o_sends):
        for send in sends:
            send.wait_send()


def shards(
    n, queries, draft_keys, draft_values, parents, private_keys, private_values,
    priv_lengths, prefix_keys, prefix_values, out_weight,
):
    blocks = n // KVH
    lh = HEADS // n
    draft = queries.shape[0]
    gr = GH * draft
    lr = lh * draft
    slots = private_keys.shape[1]
    span = prefix_keys.shape[1]
    d, cols = out_weight.shape
    vm = pl.BlockSpec(memory_space=pltpu.VMEM)
    sm = pl.BlockSpec(memory_space=pltpu.SMEM)
    hb = pl.BlockSpec(memory_space=pl.ANY)
    dma = pltpu.SemaphoreType.DMA
    return pl.pallas_call(
        functools.partial(kernel, n),
        out_shape=jax.ShapeDtypeStruct((draft, n * cols), F32),
        in_specs=[vm, vm, vm, sm, sm, hb, hb, hb, hb, hb],
        out_specs=vm,
        scratch_shapes=[
            pltpu.VMEM((slots, KVH * HD), BF16),
            pltpu.VMEM((slots, KVH * HD), BF16),
            pltpu.VMEM((span, HD), BF16),
            pltpu.VMEM((span, 2 * HD), BF16),
            pltpu.VMEM((d, cols), BF16),
            pltpu.VMEM((KVH, gr, HD), F32),
            pltpu.VMEM((KVH, gr, HD), BF16),
            pltpu.VMEM((n, gr, HD), BF16),
            pltpu.VMEM((16, KVH * HD), F32),
            pltpu.VMEM((16, KVH * HD), F32),
            pltpu.VMEM((KVH, gr, 2 * HD), F32),
            pltpu.VMEM((n, lr, 2 * HD), F32),
            pltpu.VMEM((n * gr, HD), F32),
            pltpu.VMEM((n, gr, 2 * HD), F32),
            pltpu.VMEM((blocks, n, lr, 2 * HD), F32),
            pltpu.VMEM((n, lr, HD), F32),
            pltpu.VMEM((n * draft, lh * HD), F32),
            pltpu.VMEM((n, n * draft, lh * HD), BF16),
            pltpu.VMEM((n * draft, cols), F32),
            pltpu.VMEM((n, draft, cols), F32),
            dma((5,)),
            dma((n,)), dma((n,)), dma((n,)), dma((n,)),
            dma((blocks,)), dma((blocks,)),
            dma((n,)), dma((n,)), dma((n,)), dma((n,)),
        ],
        compiler_params=pltpu.CompilerParams(
            collective_id=0, has_side_effects=True, vmem_limit_bytes=58 << 20
        ),
        cost_estimate=pl.CostEstimate(
            flops=4 * n * gr * span * HD, bytes_accessed=24 << 20, transcendentals=n * gr * span
        ),
    )(
        queries, draft_keys, draft_values, parents, priv_lengths,
        private_keys, private_values, prefix_keys, prefix_values, out_weight,
    )


def solution(mesh):
    both = ("groups", "seq")
    in_specs = (
        P(both, None), P(both, None), P(both, None), P(both),
        P(both, None, None), P(both, None, None), P(both),
        P(both, None, None), P(both, None, None), P(None, "seq"),
    )
    return jax.shard_map(
        functools.partial(shards, mesh.shape["seq"]),
        mesh=mesh, in_specs=in_specs, out_specs=P(both, None), check_vma=False,
    )
```

```python
import functools
import math

import jax
import jax.numpy as jnp
from jax import lax
from jax.experimental import pallas as pl
from jax.experimental.pallas import tpu as pltpu
from jax.sharding import PartitionSpec as P

HEADS = 64
KVH = 8
HD = 128
GH = HEADS // KVH
PARTS = 2
MESH = pl.DeviceIdType.MESH
F32 = jnp.float32
BF16 = jnp.bfloat16


def kernel(
    n,
    q_ref,
    dk_ref,
    dv_ref,
    par_ref,
    len_ref,
    pk_hbm,
    pv_hbm,
    k_hbm,
    v_hbm,
    w_hbm,
    o_ref,
    pk,
    pv,
    k,
    v,
    w,
    qf,
    qs,
    qbuf,
    dk_pad,
    dv_pad,
    priv_send,
    priv_buf,
    part,
    merge_buf,
    fin,
    att,
    gat,
    col_f,
    col,
    obuf,
    load_sem,
    q_ssem,
    q_rsem,
    p_ssem,
    p_rsem,
    m_ssem,
    m_rsem,
    g_ssem,
    g_rsem,
    o_ssem,
    o_rsem,
):
    me = lax.axis_index("seq")
    blocks = n // KVH
    lh = HEADS // n
    draft = q_ref.shape[0]
    gr = GH * draft
    lr = lh * draft
    lc = lh * HD
    cols = w.shape[1]
    g_me = me // blocks
    b_me = me % blocks
    rp = n // PARTS
    c2 = HD**-0.5 * math.log2(math.e)

    loads = [
        pltpu.make_async_copy(pk_hbm.at[0], pk, load_sem.at[0]),
        pltpu.make_async_copy(pv_hbm.at[0], pv, load_sem.at[1]),
        pltpu.make_async_copy(k_hbm.at[0], k, load_sem.at[2]),
        pltpu.make_async_copy(v_hbm.at[0], v.at[:, pl.ds(0, HD)], load_sem.at[3]),
        pltpu.make_async_copy(w_hbm, w, load_sem.at[4]),
    ]
    for load in loads[:4]:
        load.start()

    def pos(r):
        return r % PARTS * rp + r // PARTS

    here = pos(me)

    def remote(src, dst, ssem, rsem, to):
        return pltpu.make_async_remote_copy(
            src_ref=src, dst_ref=dst, send_sem=ssem, recv_sem=rsem,
            device_id={"seq": to}, device_id_type=MESH,
        )

    barrier = pltpu.get_barrier_semaphore()
    for off in range(1, n):
        pl.semaphore_signal(
            barrier, inc=1, device_id={"seq": lax.rem(me + off, n)}, device_id_type=MESH
        )
    for g in range(KVH):
        for h in range(GH):
            at = (g * GH + h) * HD
            qf[g, h * draft : (h + 1) * draft, :] = q_ref[:, at : at + HD].astype(F32)
        qs[g] = qf[g].astype(BF16)
    dk_pad[...] = jnp.zeros_like(dk_pad)
    dv_pad[...] = jnp.zeros_like(dv_pad)
    dk_pad[0:draft, :] = dk_ref[...].astype(F32)
    dv_pad[0:draft, :] = dv_ref[...].astype(F32)
    qbuf[here] = qs[g_me]
    pl.semaphore_wait(barrier, n - 1)

    q_sends = []
    for off in range(1, n):
        to = lax.rem(me + off, n)
        q_sends.append(
            remote(qs.at[to // blocks], qbuf.at[here], q_ssem.at[off], q_rsem.at[me], to)
        )
        q_sends[-1].start()
    loads[4].start()

    v[:, HD:] = jnp.ones((v.shape[0], HD), BF16)

    pad = dk_pad.shape[0]
    row_i = lax.broadcasted_iota(jnp.int32, (gr, pad), 0) % draft
    col_j = lax.broadcasted_iota(jnp.int32, (gr, pad), 1)
    seen = [[None] * draft for _ in range(draft)]
    visible = (row_i == col_j).astype(jnp.int32)
    for i in range(draft):
        for j in range(i):
            hit = (par_ref[i] == j).astype(jnp.int32)
            for mid in range(j + 1, i):
                hit = hit + (par_ref[i] == mid).astype(jnp.int32) * seen[mid][j]
            seen[i][j] = hit
            visible = jnp.where((row_i == i) & (col_j == j), hit, visible)
    slots = pk.shape[0]
    live = lax.broadcasted_iota(jnp.int32, (gr, slots), 1) < len_ref[0]
    lane = lax.broadcasted_iota(jnp.int32, (gr, HD), 1)
    loads[0].wait()
    loads[1].wait()
    nt = (((1,), (1,)), ((), ()))
    for g in range(KVH):
        cs = slice(g * HD, (g + 1) * HD)
        qg = qs[g]
        s = lax.dot_general(qg, pk[:, cs], nt, preferred_element_type=F32)
        t = lax.dot_general(qg, dk_pad[:, cs].astype(BF16), nt, preferred_element_type=F32)
        s = jnp.where(live, s, -1e30)
        t = jnp.where(visible > 0, t, -1e30)
        mx = jnp.maximum(
            jnp.max(s, axis=1, keepdims=True), jnp.max(t, axis=1, keepdims=True)
        )
        ps = jnp.exp2((s - mx) * c2)
        pt = jnp.exp2((t - mx) * c2)
        sm = jnp.sum(ps, axis=1, keepdims=True) + jnp.sum(pt, axis=1, keepdims=True)
        mix = jnp.dot(ps.astype(BF16), pv[:, cs], preferred_element_type=F32)
        mix = mix + jnp.dot(
            pt.astype(BF16), dv_pad[:, cs].astype(BF16), preferred_element_type=F32
        )
        priv_send[g, :, 0:HD] = mix
        priv_send[g, :, HD:] = jnp.where(lane == 0, mx, sm)

    def own_rows(b):
        return pl.ds(pl.multiple_of(b * lr, lr), lr)

    p_sends = []
    for off in range(1, n):
        to = lax.rem(me + off, n)
        p_sends.append(
            remote(
                priv_send.at[to // blocks, own_rows(to % blocks)], priv_buf.at[here],
                p_ssem.at[off], p_rsem.at[me], to,
            )
        )
        p_sends[-1].start()
    priv_buf[here] = priv_send[g_me, own_rows(b_me), :]

    for off in range(1, n):
        src = lax.rem(me + off, n)
        remote(qs.at[0], qbuf.at[pos(src)], q_ssem.at[off], q_rsem.at[src], src).wait_recv()
    loads[2].wait()
    loads[3].wait()
    rows = n * gr
    rb = 128
    ch = 4096
    reqs = rb // gr
    lane_b = lax.broadcasted_iota(jnp.int32, (rb, HD), 1)

    def merge_copies(p):
        ps = pl.ds(p * rp, rp)
        copies = []
        for off in range(1, blocks):
            b_to = lax.rem(b_me + off, blocks)
            copies.append(
                remote(
                    part.at[ps, own_rows(b_to)], merge_buf.at[b_me, ps],
                    m_ssem.at[p, off], m_rsem.at[p, b_me], g_me * blocks + b_to,
                )
            )
        return copies

    def merge_send(p):
        for copy in merge_copies(p):
            copy.start()

    core = me % 2
    chip = me // 2
    line = chip // 2
    side = chip % 2
    lines = n // 4

    def dev(line_at, side_at, core_at):
        return (line_at * 2 + side_at) * 2 + core_at

    across = dev(line, 1 - side, core)
    partner = dev(line, side, 1 - core)
    along = [lax.rem(line + off, lines) for off in range(1, lines)]
    mine_z = [dev(at, side, core) for at in along]
    mine_y = [dev(at, 1 - side, core) for at in [line] + along]
    other = [dev(at, sd, 1 - core) for sd in (side, 1 - side) for at in [line] + along]

    def gather_copies(p):
        pairs = [(me, across)] + [(me, to) for to in mine_z] + [(me, partner)]
        for src in mine_z:
            pairs += [(src, across), (src, partner)]
        pairs += [(src, partner) for src in mine_y]
        return [
            remote(gat.at[p, src], gat.at[p, src], g_ssem.at[p, i], g_rsem.at[p, src], to)
            for i, (src, to) in enumerate(pairs)
        ]

    def arrived(p, src):
        remote(
            gat.at[p, src], gat.at[p, src], g_ssem.at[p, 0], g_rsem.at[p, src], partner
        ).wait_recv()

    def finish(p):
        if p == 0:
            for off in range(1, n):
                src = lax.rem(me + off, n)
                remote(
                    priv_send.at[0, own_rows(0)], priv_buf.at[pos(src)],
                    p_ssem.at[off], p_rsem.at[src], src,
                ).wait_recv()
        ps = pl.ds(p * rp, rp)
        pieces = [priv_buf[ps], part[ps, own_rows(b_me), :]]
        for off in range(1, blocks):
            b_src = lax.rem(b_me + off, blocks)
            remote(
                part.at[ps, own_rows(0)], merge_buf.at[b_src, ps],
                m_ssem.at[p, off], m_rsem.at[p, b_src], g_me * blocks + b_src,
            ).wait_recv()
            pieces.append(merge_buf[b_src, ps])
        pieces = [x.reshape(rp * lr, 2 * HD) for x in pieces]
        peak = functools.reduce(jnp.maximum, [x[:, HD : HD + 1] for x in pieces])
        facs = [jnp.exp2((x[:, HD : HD + 1] - peak) * c2) for x in pieces]
        den = sum(f * x[:, HD + 1 : HD + 2] for f, x in zip(facs, pieces))
        num = sum(f * x[:, 0:HD] for f, x in zip(facs, pieces))
        fin[...] = (num / den).reshape(rp, lr, HD)
        for r in range(rp):
            for h in range(lh):
                att[r * draft : (r + 1) * draft, h * HD : (h + 1) * HD] = fin[
                    r, h * draft : (h + 1) * draft, :
                ]
        gat[p, me] = att[...].astype(BF16)
        for copy in gather_copies(p)[: lines + 1]:
            copy.start()

    def block(r, _):
        at = pl.ds(pl.multiple_of(r * reqs, reqs), reqs)
        qr = qbuf[at].reshape(rb, HD)
        peaks, mixes = [], []
        for c in range(k.shape[0] // ch):
            s = lax.dot_general(
                qr, k[c * ch : (c + 1) * ch, :], nt, preferred_element_type=F32
            )
            peaks.append(jnp.max(s, axis=1, keepdims=True))
            p = jnp.exp2((s - peaks[-1]) * c2).astype(BF16)
            mixes.append(jnp.dot(p, v[c * ch : (c + 1) * ch, :], preferred_element_type=F32))
        peak = functools.reduce(jnp.maximum, peaks)
        mix = sum(jnp.exp2((a - peak) * c2) * b for a, b in zip(peaks, mixes))
        part[at, :, 0:HD] = mix[:, 0:HD].reshape(reqs, gr, HD)
        part[at, :, HD:] = jnp.where(lane_b == 0, peak, mix[:, HD:]).reshape(reqs, gr, HD)

        @pl.when(r == half - 1)
        def _():
            merge_send(0)

        @pl.when(r == half)
        def _():
            finish(0)

        return 0

    half = rows // rb // PARTS
    lax.fori_loop(0, rows // rb, block, 0)

    def project(p, sources):
        total = None
        for src in sources:
            ws = pl.ds(pl.multiple_of(src * lc, lc), lc)
            one = jnp.dot(gat[p, src], w[ws, :], preferred_element_type=F32)
            total = one if total is None else total + one
        return total

    def forward_z(p):
        copies = gather_copies(p)[lines + 1 :]
        for i, src in enumerate(mine_z):
            arrived(p, src)
            copies[2 * i].start()
            copies[2 * i + 1].start()

    def forward_y(p):
        copies = gather_copies(p)[lines + 1 + 2 * len(mine_z) :]
        for i, src in enumerate(mine_y):
            arrived(p, src)
            copies[i].start()

    def out_copy(to, at):
        return remote(col.at[at], obuf.at[me], o_ssem.at[to], o_rsem.at[me], to)

    def out_send(p, total):
        for j in range(rp):
            q = p * rp + j
            for c in range(cols // HD):
                col_f[q, c * draft : (c + 1) * draft, :] = total[
                    j * draft : (j + 1) * draft, c * HD : (c + 1) * HD
                ]
            col[q] = col_f[q].astype(BF16)
        for j in range(rp):
            to = j * PARTS + p

            @pl.when(to != me)
            def _():
                out_copy(to, p * rp + j).start()

    merge_send(1)
    forward_z(0)
    finish(1)
    forward_y(0)
    loads[4].wait()
    total_0 = project(0, [me] + mine_z)
    forward_z(1)
    total_0 = total_0 + project(0, mine_y)
    for src in other:
        arrived(0, src)
    out_send(0, total_0 + project(0, other))
    total_1 = project(1, [me] + mine_z)
    forward_y(1)
    total_1 = total_1 + project(1, mine_y)
    for src in other:
        arrived(1, src)
    out_send(1, total_1 + project(1, other))
    obuf[me] = col[here]
    for off in range(1, n):
        src = lax.rem(me + off, n)
        remote(col.at[0], obuf.at[src], o_ssem.at[src], o_rsem.at[src], src).wait_recv()
    for src in range(n):
        got = obuf[src].astype(F32)
        for c in range(cols // HD):
            o_ref[:, src * cols + c * HD : src * cols + (c + 1) * HD] = got[
                c * draft : (c + 1) * draft, :
            ]
    for sends in (q_sends, p_sends):
        for send in sends:
            send.wait_send()
    for p in range(PARTS):
        for copy in merge_copies(p) + gather_copies(p):
            copy.wait_send()
    for off in range(1, n):
        out_copy(lax.rem(me + off, n), 0).wait_send()


def shards(
    n, queries, draft_keys, draft_values, parents, private_keys, private_values,
    priv_lengths, prefix_keys, prefix_values, out_weight,
):
    blocks = n // KVH
    lh = HEADS // n
    draft = queries.shape[0]
    gr = GH * draft
    lr = lh * draft
    slots = private_keys.shape[1]
    span = prefix_keys.shape[1]
    d, cols = out_weight.shape
    out_rows = max(16, draft * cols // HD)
    vm = pl.BlockSpec(memory_space=pltpu.VMEM)
    sm = pl.BlockSpec(memory_space=pltpu.SMEM)
    hb = pl.BlockSpec(memory_space=pl.ANY)
    dma = pltpu.SemaphoreType.DMA
    return pl.pallas_call(
        functools.partial(kernel, n),
        out_shape=jax.ShapeDtypeStruct((draft, n * cols), F32),
        in_specs=[vm, vm, vm, sm, sm, hb, hb, hb, hb, hb],
        out_specs=vm,
        scratch_shapes=[
            pltpu.VMEM((slots, KVH * HD), BF16),
            pltpu.VMEM((slots, KVH * HD), BF16),
            pltpu.VMEM((span, HD), BF16),
            pltpu.VMEM((span, 2 * HD), BF16),
            pltpu.VMEM((d, cols), BF16),
            pltpu.VMEM((KVH, gr, HD), F32),
            pltpu.VMEM((KVH, gr, HD), BF16),
            pltpu.VMEM((n, gr, HD), BF16),
            pltpu.VMEM((16, KVH * HD), F32),
            pltpu.VMEM((16, KVH * HD), F32),
            pltpu.VMEM((KVH, gr, 2 * HD), F32),
            pltpu.VMEM((n, lr, 2 * HD), F32),
            pltpu.VMEM((n, gr, 2 * HD), F32),
            pltpu.VMEM((blocks, n, lr, 2 * HD), F32),
            pltpu.VMEM((n // PARTS, lr, HD), F32),
            pltpu.VMEM((n // PARTS * draft, lh * HD), F32),
            pltpu.VMEM((PARTS, n, n // PARTS * draft, lh * HD), BF16),
            pltpu.VMEM((n, out_rows, HD), F32),
            pltpu.VMEM((n, out_rows, HD), BF16),
            pltpu.VMEM((n, out_rows, HD), BF16),
            dma((5,)),
            dma((n,)), dma((n,)), dma((n,)), dma((n,)),
            dma((PARTS, blocks)), dma((PARTS, blocks)),
            dma((PARTS, n)), dma((PARTS, n)), dma((n,)), dma((n,)),
        ],
        compiler_params=pltpu.CompilerParams(
            collective_id=0, has_side_effects=True, vmem_limit_bytes=58 << 20
        ),
        cost_estimate=pl.CostEstimate(
            flops=4 * n * gr * span * HD, bytes_accessed=24 << 20, transcendentals=n * gr * span
        ),
    )(
        queries, draft_keys, draft_values, parents, priv_lengths,
        private_keys, private_values, prefix_keys, prefix_values, out_weight,
    )


def solution(mesh):
    both = ("groups", "seq")
    in_specs = (
        P(both, None), P(both, None), P(both, None), P(both),
        P(both, None, None), P(both, None, None), P(both),
        P(both, None, None), P(both, None, None), P(None, "seq"),
    )
    return jax.shard_map(
        functools.partial(shards, mesh.shape["seq"]),
        mesh=mesh, in_specs=in_specs, out_specs=P(both, None), check_vma=False,
    )
```

```python
import functools
import math

import jax
import jax.numpy as jnp
from jax import lax
from jax.experimental import pallas as pl
from jax.experimental.pallas import tpu as pltpu
from jax.sharding import PartitionSpec as P

HEADS = 64
KVH = 8
HD = 128
GH = HEADS // KVH
PARTS = 2
MESH = pl.DeviceIdType.MESH
F32 = jnp.float32
BF16 = jnp.bfloat16


def kernel(
    n,
    q_ref,
    dk_ref,
    dv_ref,
    par_ref,
    len_ref,
    pk_hbm,
    pv_hbm,
    k_hbm,
    v_hbm,
    w_hbm,
    o_ref,
    pk,
    pv,
    k,
    v,
    w,
    qf,
    qs,
    qbuf,
    dk_pad,
    dv_pad,
    priv_send,
    priv_buf,
    part,
    merge_buf,
    fin,
    att,
    gat,
    col_f,
    col,
    obuf,
    load_sem,
    q_ssem,
    q_rsem,
    p_ssem,
    p_rsem,
    m_ssem,
    m_rsem,
    g_ssem,
    g_rsem,
    o_ssem,
    o_rsem,
):
    me = lax.axis_index("seq")
    blocks = n // KVH
    lh = HEADS // n
    draft = q_ref.shape[0]
    gr = GH * draft
    lr = lh * draft
    lc = lh * HD
    cols = w.shape[1]
    g_me = me // blocks
    b_me = me % blocks
    rp = n // PARTS
    c2 = HD**-0.5 * math.log2(math.e)

    loads = [
        pltpu.make_async_copy(pk_hbm.at[0], pk, load_sem.at[0]),
        pltpu.make_async_copy(pv_hbm.at[0], pv, load_sem.at[1]),
        pltpu.make_async_copy(k_hbm.at[0], k, load_sem.at[2]),
        pltpu.make_async_copy(v_hbm.at[0], v.at[:, pl.ds(0, HD)], load_sem.at[3]),
        pltpu.make_async_copy(w_hbm, w, load_sem.at[4]),
    ]
    for load in loads[:4]:
        load.start()

    def pos(r):
        return r % PARTS * rp + r // PARTS

    here = pos(me)

    def remote(src, dst, ssem, rsem, to):
        return pltpu.make_async_remote_copy(
            src_ref=src, dst_ref=dst, send_sem=ssem, recv_sem=rsem,
            device_id={"seq": to}, device_id_type=MESH,
        )

    barrier = pltpu.get_barrier_semaphore()
    for off in range(1, n):
        pl.semaphore_signal(
            barrier, inc=1, device_id={"seq": lax.rem(me + off, n)}, device_id_type=MESH
        )
    for g in range(KVH):
        for h in range(GH):
            at = (g * GH + h) * HD
            qf[g, h * draft : (h + 1) * draft, :] = q_ref[:, at : at + HD].astype(F32)
        qs[g] = qf[g].astype(BF16)
    dk_pad[...] = jnp.zeros_like(dk_pad)
    dv_pad[...] = jnp.zeros_like(dv_pad)
    dk_pad[0:draft, :] = dk_ref[...].astype(F32)
    dv_pad[0:draft, :] = dv_ref[...].astype(F32)
    qbuf[here] = qs[g_me]
    pl.semaphore_wait(barrier, n - 1)

    q_sends = []
    for off in range(1, n):
        to = lax.rem(me + off, n)
        q_sends.append(
            remote(qs.at[to // blocks], qbuf.at[here], q_ssem.at[off], q_rsem.at[me], to)
        )
        q_sends[-1].start()
    loads[4].start()

    v[:, HD:] = jnp.ones((v.shape[0], HD), BF16)

    pad = dk_pad.shape[0]
    row_i = lax.broadcasted_iota(jnp.int32, (gr, pad), 0) % draft
    col_j = lax.broadcasted_iota(jnp.int32, (gr, pad), 1)
    seen = [[None] * draft for _ in range(draft)]
    visible = (row_i == col_j).astype(jnp.int32)
    for i in range(draft):
        for j in range(i):
            hit = (par_ref[i] == j).astype(jnp.int32)
            for mid in range(j + 1, i):
                hit = hit + (par_ref[i] == mid).astype(jnp.int32) * seen[mid][j]
            seen[i][j] = hit
            visible = jnp.where((row_i == i) & (col_j == j), hit, visible)
    slots = pk.shape[0]
    live = lax.broadcasted_iota(jnp.int32, (gr, slots), 1) < len_ref[0]
    lane = lax.broadcasted_iota(jnp.int32, (gr, HD), 1)
    loads[0].wait()
    loads[1].wait()
    nt = (((1,), (1,)), ((), ()))
    for g in range(KVH):
        cs = slice(g * HD, (g + 1) * HD)
        qg = qs[g]
        s = lax.dot_general(qg, pk[:, cs], nt, preferred_element_type=F32)
        t = lax.dot_general(qg, dk_pad[:, cs].astype(BF16), nt, preferred_element_type=F32)
        s = jnp.where(live, s, -1e30)
        t = jnp.where(visible > 0, t, -1e30)
        mx = jnp.maximum(
            jnp.max(s, axis=1, keepdims=True), jnp.max(t, axis=1, keepdims=True)
        )
        ps = jnp.exp2((s - mx) * c2)
        pt = jnp.exp2((t - mx) * c2)
        sm = jnp.sum(ps, axis=1, keepdims=True) + jnp.sum(pt, axis=1, keepdims=True)
        mix = jnp.dot(ps.astype(BF16), pv[:, cs], preferred_element_type=F32)
        mix = mix + jnp.dot(
            pt.astype(BF16), dv_pad[:, cs].astype(BF16), preferred_element_type=F32
        )
        priv_send[g, :, 0:HD] = mix
        priv_send[g, :, HD:] = jnp.where(lane == 0, mx, sm)

    def own_rows(b):
        return pl.ds(pl.multiple_of(b * lr, lr), lr)

    p_sends = []
    for off in range(1, n):
        to = lax.rem(me + off, n)
        p_sends.append(
            remote(
                priv_send.at[to // blocks, own_rows(to % blocks)], priv_buf.at[here],
                p_ssem.at[off], p_rsem.at[me], to,
            )
        )
        p_sends[-1].start()
    priv_buf[here] = priv_send[g_me, own_rows(b_me), :]

    for off in range(1, n):
        src = lax.rem(me + off, n)
        remote(qs.at[0], qbuf.at[pos(src)], q_ssem.at[off], q_rsem.at[src], src).wait_recv()
    loads[2].wait()
    loads[3].wait()
    rows = n * gr
    rb = 128
    ch = 2048
    reqs = rb // gr
    lane_b = lax.broadcasted_iota(jnp.int32, (rb, HD), 1)

    def merge_copies(p):
        ps = pl.ds(p * rp, rp)
        copies = []
        for off in range(1, blocks):
            b_to = lax.rem(b_me + off, blocks)
            copies.append(
                remote(
                    part.at[ps, own_rows(b_to)], merge_buf.at[b_me, ps],
                    m_ssem.at[p, off], m_rsem.at[p, b_me], g_me * blocks + b_to,
                )
            )
        return copies

    def merge_send(p):
        for copy in merge_copies(p):
            copy.start()

    core = me % 2
    chip = me // 2
    line = chip // 2
    side = chip % 2
    lines = n // 4

    def dev(line_at, side_at, core_at):
        return (line_at * 2 + side_at) * 2 + core_at

    across = dev(line, 1 - side, core)
    partner = dev(line, side, 1 - core)
    along = [lax.rem(line + off, lines) for off in range(1, lines)]
    mine_z = [dev(at, side, core) for at in along]
    mine_y = [dev(at, 1 - side, core) for at in [line] + along]
    other = [dev(at, sd, 1 - core) for sd in (side, 1 - side) for at in [line] + along]

    def gather_copies(p):
        pairs = [(me, across)] + [(me, to) for to in mine_z] + [(me, partner)]
        for src in mine_z:
            pairs += [(src, across), (src, partner)]
        pairs += [(src, partner) for src in mine_y]
        return [
            remote(gat.at[p, src], gat.at[p, src], g_ssem.at[p, i], g_rsem.at[p, src], to)
            for i, (src, to) in enumerate(pairs)
        ]

    def arrived(p, src):
        remote(
            gat.at[p, src], gat.at[p, src], g_ssem.at[p, 0], g_rsem.at[p, src], partner
        ).wait_recv()

    def finish(p):
        if p == 0:
            for off in range(1, n):
                src = lax.rem(me + off, n)
                remote(
                    priv_send.at[0, own_rows(0)], priv_buf.at[pos(src)],
                    p_ssem.at[off], p_rsem.at[src], src,
                ).wait_recv()
        ps = pl.ds(p * rp, rp)
        pieces = [priv_buf[ps], part[ps, own_rows(b_me), :]]
        for off in range(1, blocks):
            b_src = lax.rem(b_me + off, blocks)
            remote(
                part.at[ps, own_rows(0)], merge_buf.at[b_src, ps],
                m_ssem.at[p, off], m_rsem.at[p, b_src], g_me * blocks + b_src,
            ).wait_recv()
            pieces.append(merge_buf[b_src, ps])
        pieces = [x.reshape(rp * lr, 2 * HD) for x in pieces]
        peak = functools.reduce(jnp.maximum, [x[:, HD : HD + 1] for x in pieces])
        facs = [jnp.exp2((x[:, HD : HD + 1] - peak) * c2) for x in pieces]
        den = sum(f * x[:, HD + 1 : HD + 2] for f, x in zip(facs, pieces))
        num = sum(f * x[:, 0:HD] for f, x in zip(facs, pieces))
        fin[...] = (num / den).reshape(rp, lr, HD)
        for r in range(rp):
            for h in range(lh):
                att[r * draft : (r + 1) * draft, h * HD : (h + 1) * HD] = fin[
                    r, h * draft : (h + 1) * draft, :
                ]
        gat[p, me] = att[...].astype(BF16)
        for copy in gather_copies(p)[: lines + 1]:
            copy.start()

    def block(r, _):
        at = pl.ds(pl.multiple_of(r * reqs, reqs), reqs)
        qr = qbuf[at].reshape(rb, HD)
        peaks, mixes = [], []
        for c in range(k.shape[0] // ch):
            s = lax.dot_general(
                qr, k[c * ch : (c + 1) * ch, :], nt, preferred_element_type=F32
            )
            peaks.append(jnp.max(s, axis=1, keepdims=True))
            p = jnp.exp2((s - peaks[-1]) * c2).astype(BF16)
            mixes.append(jnp.dot(p, v[c * ch : (c + 1) * ch, :], preferred_element_type=F32))
        peak = functools.reduce(jnp.maximum, peaks)
        mix = sum(jnp.exp2((a - peak) * c2) * b for a, b in zip(peaks, mixes))
        part[at, :, 0:HD] = mix[:, 0:HD].reshape(reqs, gr, HD)
        part[at, :, HD:] = jnp.where(lane_b == 0, peak, mix[:, HD:]).reshape(reqs, gr, HD)

        @pl.when(r == half - 1)
        def _():
            merge_send(0)

        @pl.when(r == half)
        def _():
            finish(0)

        return 0

    half = rows // rb // PARTS
    lax.fori_loop(0, rows // rb, block, 0)

    def project(p, sources):
        total = None
        for src in sources:
            ws = pl.ds(pl.multiple_of(src * lc, lc), lc)
            one = jnp.dot(gat[p, src], w[ws, :], preferred_element_type=F32)
            total = one if total is None else total + one
        return total

    def forward_z(p):
        copies = gather_copies(p)[lines + 1 :]
        for i, src in enumerate(mine_z):
            arrived(p, src)
            copies[2 * i].start()
            copies[2 * i + 1].start()

    def forward_y(p):
        copies = gather_copies(p)[lines + 1 + 2 * len(mine_z) :]
        for i, src in enumerate(mine_y):
            arrived(p, src)
            copies[i].start()

    def out_copy(to, at):
        return remote(col.at[at], obuf.at[me], o_ssem.at[to], o_rsem.at[me], to)

    def out_send(p, total):
        for j in range(rp):
            q = p * rp + j
            for c in range(cols // HD):
                col_f[q, c * draft : (c + 1) * draft, :] = total[
                    j * draft : (j + 1) * draft, c * HD : (c + 1) * HD
                ]
            col[q] = col_f[q].astype(BF16)
        for j in range(rp):
            to = j * PARTS + p

            @pl.when(to != me)
            def _():
                out_copy(to, p * rp + j).start()

    merge_send(1)
    forward_z(0)
    finish(1)
    forward_y(0)
    loads[4].wait()
    total_0 = project(0, [me] + mine_z)
    forward_z(1)
    total_0 = total_0 + project(0, mine_y)
    for src in other:
        arrived(0, src)
    out_send(0, total_0 + project(0, other))
    total_1 = project(1, [me] + mine_z)
    forward_y(1)
    total_1 = total_1 + project(1, mine_y)
    for src in other:
        arrived(1, src)
    out_send(1, total_1 + project(1, other))
    obuf[me] = col[here]
    for off in range(1, n):
        src = lax.rem(me + off, n)
        remote(col.at[0], obuf.at[src], o_ssem.at[src], o_rsem.at[src], src).wait_recv()
    for src in range(n):
        got = obuf[src].astype(F32)
        for c in range(cols // HD):
            o_ref[:, src * cols + c * HD : src * cols + (c + 1) * HD] = got[
                c * draft : (c + 1) * draft, :
            ]
    for sends in (q_sends, p_sends):
        for send in sends:
            send.wait_send()
    for p in range(PARTS):
        for copy in merge_copies(p) + gather_copies(p):
            copy.wait_send()
    for off in range(1, n):
        out_copy(lax.rem(me + off, n), 0).wait_send()


def shards(
    n, queries, draft_keys, draft_values, parents, private_keys, private_values,
    priv_lengths, prefix_keys, prefix_values, out_weight,
):
    blocks = n // KVH
    lh = HEADS // n
    draft = queries.shape[0]
    gr = GH * draft
    lr = lh * draft
    slots = private_keys.shape[1]
    span = prefix_keys.shape[1]
    d, cols = out_weight.shape
    out_rows = max(16, draft * cols // HD)
    vm = pl.BlockSpec(memory_space=pltpu.VMEM)
    sm = pl.BlockSpec(memory_space=pltpu.SMEM)
    hb = pl.BlockSpec(memory_space=pl.ANY)
    dma = pltpu.SemaphoreType.DMA
    return pl.pallas_call(
        functools.partial(kernel, n),
        out_shape=jax.ShapeDtypeStruct((draft, n * cols), F32),
        in_specs=[vm, vm, vm, sm, sm, hb, hb, hb, hb, hb],
        out_specs=vm,
        scratch_shapes=[
            pltpu.VMEM((slots, KVH * HD), BF16),
            pltpu.VMEM((slots, KVH * HD), BF16),
            pltpu.VMEM((span, HD), BF16),
            pltpu.VMEM((span, 2 * HD), BF16),
            pltpu.VMEM((d, cols), BF16),
            pltpu.VMEM((KVH, gr, HD), F32),
            pltpu.VMEM((KVH, gr, HD), BF16),
            pltpu.VMEM((n, gr, HD), BF16),
            pltpu.VMEM((16, KVH * HD), F32),
            pltpu.VMEM((16, KVH * HD), F32),
            pltpu.VMEM((KVH, gr, 2 * HD), F32),
            pltpu.VMEM((n, lr, 2 * HD), F32),
            pltpu.VMEM((n, gr, 2 * HD), F32),
            pltpu.VMEM((blocks, n, lr, 2 * HD), F32),
            pltpu.VMEM((n // PARTS, lr, HD), F32),
            pltpu.VMEM((n // PARTS * draft, lh * HD), F32),
            pltpu.VMEM((PARTS, n, n // PARTS * draft, lh * HD), BF16),
            pltpu.VMEM((n, out_rows, HD), F32),
            pltpu.VMEM((n, out_rows, HD), BF16),
            pltpu.VMEM((n, out_rows, HD), BF16),
            dma((5,)),
            dma((n,)), dma((n,)), dma((n,)), dma((n,)),
            dma((PARTS, blocks)), dma((PARTS, blocks)),
            dma((PARTS, n)), dma((PARTS, n)), dma((n,)), dma((n,)),
        ],
        compiler_params=pltpu.CompilerParams(
            collective_id=0, has_side_effects=True, vmem_limit_bytes=58 << 20
        ),
        cost_estimate=pl.CostEstimate(
            flops=4 * n * gr * span * HD, bytes_accessed=24 << 20, transcendentals=n * gr * span
        ),
    )(
        queries, draft_keys, draft_values, parents, priv_lengths,
        private_keys, private_values, prefix_keys, prefix_values, out_weight,
    )


def solution(mesh):
    both = ("groups", "seq")
    in_specs = (
        P(both, None), P(both, None), P(both, None), P(both),
        P(both, None, None), P(both, None, None), P(both),
        P(both, None, None), P(both, None, None), P(None, "seq"),
    )
    return jax.shard_map(
        functools.partial(shards, mesh.shape["seq"]),
        mesh=mesh, in_specs=in_specs, out_specs=P(both, None), check_vma=False,
    )
```
